32 devices in a mesh: sect: 2 (over y), node: 4 (over z), fn: 2 (over x), sub: 2 (over core).
Axes of the slice: x: 2, y: 2, z: 4, core: 2. Of those that a mesh axis runs over, the one named last changes fastest.
Arguments:
- volume_grad: bfloat16 [2048, 32, 128], P(('sect', 'node', 'fn', 'sub')), parts along dimension 0, may hold values from -0.5 to 0.5
- volume_coords: float32 [2048, 3, 128], P(('sect', 'node', 'fn', 'sub')), parts along dimension 0, may hold values from -2.1366198 to 3
- support: int32 [2048, 32], P(('sect', 'node', 'fn', 'sub')), parts along dimension 0, may hold values from 0 to 31
- control_coords: float32 [64, 3, 128], P(('sect', 'node')), parts along dimension 0, may hold values from -2.1366198 to 3
- neighbours: int32 [64, 4], P(('sect', 'node')), parts along dimension 0, may hold values from 0 to 31
- block_inverse: float32 [64, 128, 128], P(('sect', 'node')), parts along dimension 0, may hold values from -0.09375 to 0.09375
Outputs:
- control_gradient: float32 [64, 32, 128], P(('sect', 'node')), parts along dimension 0
- adjoint: float32 [64, 32, 128], P(('sect', 'node')), parts along dimension 0
The draws below stay inside these ranges and needn't reach their ends.
There are 2 independent parts, one for each index of `sect`. The reference program is written for one: setup_inputs(seed, part) draws one part's arguments, and reference() takes and returns one part's arrays. A program takes and returns all parts, laid end to end along the dimension named above; each array names one. Nothing has to cross between parts.
All inputs are finite; a program needn't handle non-finite values.
Results may differ from the reference program's by a relative error of at most 0.0034.
Values may be sent and summed in bfloat16 or wider, within the bound.
A program may use at most 64 MiB of HBM per device.

```python
import math
import jax
import jax.numpy as jnp
from jax import lax

FUNC = 32
BLOCK = 128
SUPPORT = 32
COUPLED = 4
SWEEPS = 2
NSB = 1024
NCB = 32


ARC_LENGTH = 4.0


AXIAL_DEPTH = 3.0


LAYER_THICKNESS = 1.5


def cycle_shape():
    window = min(SUPPORT, NCB)
    spacing = ARC_LENGTH / window
    cycle_radius = NCB * spacing / (2.0 * math.pi)
    return (window, spacing, cycle_radius)


def cycle_positions(key):
    return jax.random.permutation(jax.random.fold_in(key, 101), NCB).astype(jnp.int32)


def cycle_holder(key):
    positions = cycle_positions(key)
    return jnp.zeros((NCB,), jnp.int32).at[positions].set(jnp.arange(NCB, dtype=jnp.int32))


def window_centers(key):
    first_starts = jax.random.permutation(jax.random.fold_in(key, 202), NCB).astype(jnp.int32)
    random_starts = jax.random.randint(jax.random.fold_in(key, 303), (NSB,), 0, NCB, dtype=jnp.int32)
    shell_index = jnp.arange(NSB, dtype=jnp.int32)
    return jnp.where(shell_index < NCB, first_starts[shell_index % NCB], random_starts)


def draw_support(key, part):
    window, spacing, cycle_radius = cycle_shape()
    holder = cycle_holder(key)
    centers = window_centers(key)
    listed = jnp.arange(SUPPORT, dtype=jnp.int32) % window - window // 2
    cycle_slots = (centers[:, None] + listed[None, :]) % NCB
    return holder[cycle_slots]


def draw_volume_coords(key, part):
    window, spacing, cycle_radius = cycle_shape()
    centers = window_centers(key).astype(jnp.float32)
    along = jax.random.uniform(jax.random.fold_in(key, 404), (NSB, BLOCK), jnp.float32)
    across = jax.random.uniform(jax.random.fold_in(key, 505), (NSB, BLOCK), jnp.float32)
    height = jax.random.uniform(jax.random.fold_in(key, 606), (NSB, BLOCK), jnp.float32)
    arc_place = centers[:, None] * spacing + ARC_LENGTH * (along - 0.5)
    angle = arc_place / cycle_radius
    radial = cycle_radius + LAYER_THICKNESS * across
    return jnp.stack([radial * jnp.cos(angle), radial * jnp.sin(angle), AXIAL_DEPTH * height], axis=1)


def draw_control_coords(key, part):
    window, spacing, cycle_radius = cycle_shape()
    positions = cycle_positions(key).astype(jnp.float32)
    along = jax.random.uniform(jax.random.fold_in(key, 707), (NCB, BLOCK), jnp.float32)
    height = jax.random.uniform(jax.random.fold_in(key, 808), (NCB, BLOCK), jnp.float32)
    surface = jax.random.uniform(jax.random.fold_in(key, 909), (NCB, BLOCK), jnp.float32)
    shock_share = 0.5
    on_shock = jnp.where(surface < shock_share, 1.0, 0.0)
    arc_place = (positions[:, None] + 0.5) * spacing + ARC_LENGTH * (along - 0.5)
    angle = arc_place / cycle_radius
    radial = cycle_radius + LAYER_THICKNESS * on_shock
    return jnp.stack([radial * jnp.cos(angle), radial * jnp.sin(angle), AXIAL_DEPTH * height], axis=1)


def draw_neighbours(key, part):
    window, spacing, cycle_radius = cycle_shape()
    positions = cycle_positions(key)
    holder = cycle_holder(key)
    reach_most = max(1, window // 2)
    steps_away = jax.random.randint(jax.random.fold_in(key, 111), (NCB, COUPLED), 1, reach_most + 1, dtype=jnp.int32)
    signs_drawn = jax.random.randint(jax.random.fold_in(key, 222), (NCB, COUPLED), 0, 2, dtype=jnp.int32) * 2 - 1
    offsets = steps_away * signs_drawn
    offsets = offsets.at[:, 0].set(1)
    return holder[(positions[:, None] + offsets) % NCB]


def level_of(key, extent, split, low, largest):
    def one(axis_at, parts):
        draws = jax.random.uniform(jax.random.fold_in(jax.random.fold_in(key, 6), axis_at), (parts,), jnp.float32, low / len(split), largest / len(split))
        return jnp.repeat(jnp.exp(draws), extent[axis_at] // parts).reshape((-1,) + (1,) * (len(extent) - axis_at - 1))

    loudness = one(*split[0])
    for cut in split[1:]:
        loudness = loudness * one(*cut)
    return loudness


def normal_values(rng, shape, spread, bound, cuts=(), kind=jnp.bfloat16):
    gain = level_of(rng, shape, cuts, -0.22, 0.18) if cuts else 1.0
    values = jax.random.normal(rng, shape, jnp.float32) * spread * gain
    return jnp.minimum(jnp.maximum(values, -bound), bound).astype(kind)


def setup_inputs(seed: int = 0, part: int = 0) -> dict:
    key_list = jax.random.split(jax.random.key(seed), 7)
    part_splits = jax.random.split(jax.random.fold_in(key_list[6], part), 7)
    volume_grad = normal_values(part_splits[0], (NSB, FUNC, BLOCK), (12.0 / (NSB * SUPPORT * BLOCK / NCB) ** 0.5), 0.5, ((0, 16),))
    volume_coords = draw_volume_coords(jax.random.fold_in(jax.random.fold_in(key_list[6], part), 71), part)
    support = draw_support(jax.random.fold_in(jax.random.fold_in(key_list[6], part), 71), part)
    control_coords = draw_control_coords(jax.random.fold_in(jax.random.fold_in(key_list[6], part), 71), part)
    neighbours = draw_neighbours(jax.random.fold_in(jax.random.fold_in(key_list[6], part), 71), part)
    block_inverse = normal_values(part_splits[5], (NCB, BLOCK, BLOCK), 4096 ** -0.5, 0.09375, ((0, 4),), jnp.float32)
    return dict(volume_grad=volume_grad, volume_coords=volume_coords, support=support, control_coords=control_coords, neighbours=neighbours, block_inverse=block_inverse)


RADIUS = 1.2

def wendland(points, centers):
    diff = points[..., :, :, None] - centers[..., :, None, :]
    dist = jnp.sqrt(lax.optimization_barrier(jnp.sum(diff * diff, axis=-3)))
    ratio = dist / RADIUS
    inside = jnp.maximum(1.0 - ratio, 0.0)
    return (inside ** 4 * (4.0 * ratio + 1.0)).astype(jnp.bfloat16)

def reference(volume_grad, volume_coords, support, control_coords, neighbours, block_inverse):
    group = 32
    count = volume_grad.shape[0] // group
    grads = volume_grad.reshape(count, group, FUNC, BLOCK)
    coords = volume_coords.reshape(count, group, 3, BLOCK)
    lists = support.reshape(count, group, SUPPORT)

    def step(total, items):
        block_grads, block_coords, block_lists = items
        centers = control_coords[block_lists]
        tiles_phi = wendland(block_coords[:, None], centers)
        tiles = jnp.einsum('gfi,gkij->gkfj', block_grads.astype(jnp.float32), tiles_phi.astype(jnp.float32))
        total = total.at[block_lists.reshape(-1)].add(tiles.reshape(-1, FUNC, BLOCK))
        return (total, None)
    empty = jnp.zeros((NCB, FUNC, BLOCK), jnp.float32)
    control_gradient, _ = lax.scan(step, empty, (grads, coords, lists))
    adjoint = jnp.einsum('cfi,cij->cfj', control_gradient, block_inverse, precision=lax.Precision.HIGHEST)
    pair_phi = wendland(control_coords[neighbours], control_coords[:, None])
    for sweep in range(SWEEPS):
        values = adjoint.astype(jnp.bfloat16)
        near = values[neighbours]
        coupling = jnp.einsum('ckfi,ckij->cfj', near.astype(jnp.float32), pair_phi.astype(jnp.float32))
        adjoint = jnp.einsum('cfi,cij->cfj', control_gradient - coupling, block_inverse, precision=lax.Precision.HIGHEST)
    return (control_gradient, adjoint)
```

```python
import functools

import jax
import jax.numpy as jnp
from jax import lax
from jax.experimental import pallas as pl
from jax.experimental.pallas import tpu as pltpu
from jax.sharding import PartitionSpec as P

SWEEPS = 2


RADIUS = 1.2


DEPTH = 32


def wendland(points, centers):
    diff = points[..., :, :, None] - centers[..., :, None, :]
    dist = jnp.sqrt(jnp.sum(diff * diff, axis=-3))
    ratio = dist / RADIUS
    inside = jnp.maximum(1.0 - ratio, 0.0)
    return (inside**4 * (4.0 * ratio + 1.0)).astype(jnp.bfloat16)


def cut(x, terms):
    pieces = []
    for _ in range(terms):
        piece = lax.reduce_precision(x, 8, 7)
        pieces.append(piece)
        x = x - piece
    return pieces


def factors(points, left):
    high, low = cut(points * (1.0 / RADIUS), 2)
    kept = high + low
    norm = jnp.concatenate(cut(jnp.sum(kept * kept, axis=1, keepdims=True), 3), axis=1)
    one = jnp.ones_like(norm)
    if left:
        rows = [high, low, high, low, norm, one]
    else:
        rows = [-2.0 * high, -2.0 * high, -2.0 * low, -2.0 * low, one, norm]
    used = sum(row.shape[1] for row in rows)
    rows.append(jnp.zeros((points.shape[0], DEPTH - used, points.shape[2]), jnp.float32))
    return jnp.concatenate(rows, axis=1).astype(jnp.bfloat16)


def quarter_phi(square):
    square = jnp.maximum(square, 1e-12)
    ratio = square * lax.rsqrt(square)
    inside = jnp.maximum(1.0 - ratio, 0.0)
    inside = inside * inside
    return (inside * inside * (ratio + 0.25)).astype(jnp.bfloat16)


def gradient_kernel(left_ref, right_ref, grad_ref, weight_ref, out_ref):
    funcs = grad_ref.shape[0]
    width = out_ref.shape[2]
    square = jnp.dot(left_ref[...], right_ref[0], preferred_element_type=jnp.float32)
    phi = quarter_phi(square)
    grads = grad_ref[...]
    scaled = []
    for half in range(2):
        row = jnp.broadcast_to(weight_ref[0, half : half + 1, :], grads.shape)
        scaled.append(grads * row.astype(jnp.bfloat16))
    both = jnp.dot(jnp.concatenate(scaled, 0), phi, preferred_element_type=jnp.float32)
    out_ref[0] = both[:funcs, :width]
    out_ref[1] = both[funcs:, width:]


def partial_gradient(volume_grad, volume_coords, support, all_centers):
    blocks, funcs, width = volume_grad.shape
    control = all_centers.shape[0]
    pairs = control // 2
    points = blocks * width
    left = factors(volume_coords, True).transpose(0, 2, 1).reshape(points, DEPTH)
    right = factors(all_centers, False).reshape(pairs, 2, DEPTH, width)
    right = right.transpose(0, 2, 1, 3).reshape(pairs, DEPTH, 2 * width)
    grads = volume_grad.transpose(1, 0, 2).reshape(funcs, points)
    listed = support[None] == jnp.arange(control, dtype=jnp.int32)[:, None, None]
    counts = 4.0 * jnp.sum(listed.astype(jnp.float32), axis=2)
    weights = jnp.broadcast_to(counts[:, :, None], (control, blocks, width))
    weights = weights.reshape(pairs, 2, points)
    return pl.pallas_call(
        gradient_kernel,
        grid=(pairs,),
        in_specs=[
            pl.BlockSpec((points, DEPTH), lambda i: (0, 0)),
            pl.BlockSpec((1, DEPTH, 2 * width), lambda i: (i, 0, 0)),
            pl.BlockSpec((funcs, points), lambda i: (0, 0)),
            pl.BlockSpec((1, 2, points), lambda i: (i, 0, 0)),
        ],
        out_specs=pl.BlockSpec((2, funcs, width), lambda i: (i, 0, 0)),
        out_shape=jax.ShapeDtypeStruct((control, funcs, width), jnp.float32),
        compiler_params=pltpu.CompilerParams(vmem_limit_bytes=48 << 20),
    )(left, right, grads, weights)


def local(volume_grad, volume_coords, support, control_coords, neighbours, block_inverse):
    all_centers = lax.all_gather(control_coords, "node", axis=0, tiled=True)
    partial_value = partial_gradient(volume_grad, volume_coords, support, all_centers)
    owned = lax.psum_scatter(partial_value, "node", scatter_dimension=0, tiled=True)
    control_gradient = lax.psum(owned, ("fn", "sub"))
    adjoint = jnp.einsum(
        "cfi,cij->cfj", control_gradient, block_inverse, precision=lax.Precision.HIGHEST
    )
    picks = neighbours[:, :, None] == jnp.arange(all_centers.shape[0], dtype=jnp.int32)
    near_coords = jnp.einsum(
        "ckn,ndi->ckdi", picks.astype(jnp.float32), all_centers, precision=lax.Precision.HIGHEST
    )
    pair_phi = wendland(near_coords, control_coords[:, None])
    picks = picks.astype(jnp.bfloat16)
    for sweep in range(SWEEPS):
        values = lax.all_gather(adjoint.astype(jnp.bfloat16), "node", axis=0, tiled=True)
        near = jnp.einsum("ckn,nfi->ckfi", picks, values)
        coupling = jnp.einsum("ckfi,ckij->cfj", near, pair_phi, preferred_element_type=jnp.float32)
        adjoint = jnp.einsum(
            "cfi,cij->cfj",
            control_gradient - coupling,
            block_inverse,
            precision=lax.Precision.HIGHEST,
        )
    return (control_gradient, adjoint)


def solution(mesh):
    return jax.shard_map(
        local,
        mesh=mesh,
        in_specs=(
            P(("sect", "node", "fn", "sub"), None, None),
            P(("sect", "node", "fn", "sub"), None, None),
            P(("sect", "node", "fn", "sub"), None),
            P(("sect", "node"), None, None),
            P(("sect", "node"), None),
            P(("sect", "node"), None, None),
        ),
        out_specs=(P(("sect", "node"), None, None), P(("sect", "node"), None, None)),
        check_vma=False,
    )
```

```python
import functools

import jax
import jax.numpy as jnp
from jax import lax
from jax.experimental import pallas as pl
from jax.experimental.pallas import tpu as pltpu
from jax.sharding import PartitionSpec as P

SWEEPS = 2


RADIUS = 1.2


DEPTH = 32


MESH = pl.DeviceIdType.MESH


def wendland(points, centers):
    diff = points[..., :, :, None] - centers[..., :, None, :]
    dist = jnp.sqrt(jnp.sum(diff * diff, axis=-3))
    ratio = dist / RADIUS
    inside = jnp.maximum(1.0 - ratio, 0.0)
    return (inside**4 * (4.0 * ratio + 1.0)).astype(jnp.bfloat16)


def cut(x, terms):
    pieces = []
    for _ in range(terms):
        piece = lax.reduce_precision(x, 8, 7)
        pieces.append(piece)
        x = x - piece
    return pieces


def factors(points, left):
    high, low = cut(points * (1.0 / RADIUS), 2)
    kept = high + low
    norm = jnp.concatenate(cut(jnp.sum(kept * kept, axis=1, keepdims=True), 3), axis=1)
    one = jnp.ones_like(norm)
    if left:
        rows = [high, low, high, low, norm, one]
    else:
        rows = [-2.0 * high, -2.0 * high, -2.0 * low, -2.0 * low, one, norm]
    used = sum(row.shape[1] for row in rows)
    rows.append(jnp.zeros((points.shape[0], DEPTH - used, points.shape[2]), jnp.float32))
    return jnp.concatenate(rows, axis=1).astype(jnp.bfloat16)


def quarter_phi(square):
    square = jnp.maximum(square, 1e-12)
    ratio = square * lax.rsqrt(square)
    inside = jnp.maximum(1.0 - ratio, 0.0)
    inside = inside * inside
    return (inside * inside * (ratio + 0.25)).astype(jnp.bfloat16)


def gradient_kernel(left_ref, right_ref, grad_ref, weight_ref, out_ref):
    funcs = grad_ref.shape[0]
    width = out_ref.shape[2]
    square = jnp.dot(left_ref[...], right_ref[0], preferred_element_type=jnp.float32)
    phi = quarter_phi(square)
    grads = grad_ref[...]
    scaled = []
    for half in range(2):
        row = jnp.broadcast_to(weight_ref[0, half : half + 1, :], grads.shape)
        scaled.append(grads * row.astype(jnp.bfloat16))
    both = jnp.dot(jnp.concatenate(scaled, 0), phi, preferred_element_type=jnp.float32)
    out_ref[0] = both[:funcs, :width]
    out_ref[1] = both[funcs:, width:]


def partial_gradient(volume_grad, volume_coords, support, all_centers):
    blocks, funcs, width = volume_grad.shape
    control = all_centers.shape[0]
    pairs = control // 2
    points = blocks * width
    left = factors(volume_coords, True).transpose(0, 2, 1).reshape(points, DEPTH)
    right = factors(all_centers, False).reshape(pairs, 2, DEPTH, width)
    right = right.transpose(0, 2, 1, 3).reshape(pairs, DEPTH, 2 * width)
    grads = volume_grad.transpose(1, 0, 2).reshape(funcs, points)
    listed = support[None] == jnp.arange(control, dtype=jnp.int32)[:, None, None]
    counts = 4.0 * jnp.sum(listed.astype(jnp.float32), axis=2)
    weights = jnp.broadcast_to(counts[:, :, None], (control, blocks, width))
    weights = weights.reshape(pairs, 2, points)
    return pl.pallas_call(
        gradient_kernel,
        grid=(pairs,),
        in_specs=[
            pl.BlockSpec((points, DEPTH), lambda i: (0, 0)),
            pl.BlockSpec((1, DEPTH, 2 * width), lambda i: (i, 0, 0)),
            pl.BlockSpec((funcs, points), lambda i: (0, 0)),
            pl.BlockSpec((1, 2, points), lambda i: (i, 0, 0)),
        ],
        out_specs=pl.BlockSpec((2, funcs, width), lambda i: (i, 0, 0)),
        out_shape=jax.ShapeDtypeStruct((control, funcs, width), jnp.float32),
        compiler_params=pltpu.CompilerParams(vmem_limit_bytes=48 << 20),
    )(left, right, grads, weights)


def place(rank, sizes):
    copies = sizes[1] * sizes[2]
    return {
        "node": rank // copies,
        "fn": (rank % copies) // sizes[2],
        "sub": rank % sizes[2],
    }


def signal_and_wait(peers, where):
    barrier = pltpu.get_barrier_semaphore()

    def tell(step, carry):
        pl.semaphore_signal(barrier, inc=1, device_id=where(step), device_id_type=MESH)
        return carry

    lax.fori_loop(1, peers + 1, tell, 0)
    pl.semaphore_wait(barrier, peers)


def center_kernel(nodes, own_ref, all_ref, send_sem, recv_sem):
    me = lax.axis_index("node")

    def where(step):
        return {"node": (me + step) % nodes}

    signal_and_wait(nodes - 1, where)
    all_ref[me] = own_ref[...]

    def copy(step):
        return pltpu.make_async_remote_copy(
            src_ref=own_ref,
            dst_ref=all_ref.at[me],
            send_sem=send_sem.at[step],
            recv_sem=recv_sem.at[step],
            device_id=where(step),
            device_id_type=MESH,
        )

    for step in range(1, nodes):
        copy(step).start()
    for step in range(1, nodes):
        copy(step).wait()


def gather_centers(control_coords, nodes):
    own, dims, width = control_coords.shape
    gathered = pl.pallas_call(
        functools.partial(center_kernel, nodes),
        in_specs=[pl.BlockSpec(memory_space=pltpu.VMEM)],
        out_specs=pl.BlockSpec(memory_space=pltpu.VMEM),
        out_shape=jax.ShapeDtypeStruct((nodes, own * dims, width), jnp.float32),
        scratch_shapes=[
            pltpu.SemaphoreType.DMA((nodes,)),
            pltpu.SemaphoreType.DMA((nodes,)),
        ],
        compiler_params=pltpu.CompilerParams(collective_id=0, has_side_effects=True),
    )(control_coords.reshape(own * dims, width))
    return gathered.reshape(nodes * own, dims, width)


def adjoint_kernel(
    sizes,
    near_ref,
    part_ref,
    inverse_ref,
    phi_ref,
    gradient_ref,
    adjoint_ref,
    landed,
    values,
    wide,
    total,
    part_send,
    part_recv,
    gradient_send,
    gradient_recv,
    adjoint_send,
    adjoint_recv,
    value_send,
    value_recv,
):
    nodes = sizes[0]
    copies = sizes[1] * sizes[2]
    ranks = nodes * copies
    node = lax.axis_index("node")
    share = lax.axis_index("fn") * sizes[2] + lax.axis_index("sub")
    rank = node * copies + share
    own = inverse_ref.shape[0]
    rows = part_ref.shape[1] // own
    coupled = phi_ref.shape[1] // phi_ref.shape[2]
    width = phi_ref.shape[2]

    def peer(step):
        return (rank + step) % ranks

    signal_and_wait(ranks - 1, lambda step: place(peer(step), sizes))

    def part_copy(step):
        return pltpu.make_async_remote_copy(
            src_ref=part_ref.at[peer(step)],
            dst_ref=landed.at[step],
            send_sem=part_send.at[step],
            recv_sem=part_recv.at[step],
            device_id=place(peer(step), sizes),
            device_id_type=MESH,
        )

    def start_part(step, carry):
        part_copy(step).start()
        return carry

    lax.fori_loop(1, ranks, start_part, 0)
    total[...] = part_ref[rank].astype(jnp.float32)

    def add_part(step, carry):
        part_copy(step).wait_recv()
        total[...] += landed[step].astype(jnp.float32)
        return carry

    lax.fori_loop(1, ranks, add_part, 0)
    gradient_ref[share] = total[...]

    def share_copy(ref, send, recv, step):
        return pltpu.make_async_remote_copy(
            src_ref=ref.at[share],
            dst_ref=ref.at[share],
            send_sem=send.at[step],
            recv_sem=recv.at[step],
            device_id=place(node * copies + (share + step) % copies, sizes),
            device_id_type=MESH,
        )

    for step in range(1, copies):
        share_copy(gradient_ref, gradient_send, gradient_recv, step).start()

    def solve(c, coupling):
        right = total[c * rows : (c + 1) * rows, :]
        if coupling is not None:
            right = right - coupling
        return jnp.dot(
            right,
            inverse_ref[c],
            precision=lax.Precision.HIGHEST,
            preferred_element_type=jnp.float32,
        )

    def value_copy(sweep, step):
        return pltpu.make_async_remote_copy(
            src_ref=values.at[sweep, node],
            dst_ref=values.at[sweep, node],
            send_sem=value_send.at[sweep, step],
            recv_sem=value_recv.at[sweep, step],
            device_id=place(((node + step) % nodes) * copies + share, sizes),
            device_id_type=MESH,
        )

    adjoint = [solve(c, None) for c in range(own)]
    for sweep in range(SWEEPS):
        values[sweep, node] = jnp.concatenate(adjoint, 0).astype(jnp.bfloat16)
        for step in range(1, nodes):
            value_copy(sweep, step).start()
        for step in range(1, nodes):
            value_copy(sweep, step).wait_recv()
        for n in range(nodes):
            block = values[sweep, n].astype(jnp.float32)
            wide[n * own : (n + 1) * own] = block.reshape(own, rows, width)
        adjoint = []
        for c in range(own):
            near = [wide[near_ref[c, k]] for k in range(coupled)]
            near = jnp.concatenate(near, 1).astype(jnp.bfloat16)
            coupling = jnp.dot(near, phi_ref[c], preferred_element_type=jnp.float32)
            adjoint.append(solve(c, coupling))
    adjoint_ref[share] = jnp.concatenate(adjoint, 0)
    for step in range(1, copies):
        share_copy(adjoint_ref, adjoint_send, adjoint_recv, step).start()

    def end_part(step, carry):
        part_copy(step).wait_send()
        return carry

    lax.fori_loop(1, ranks, end_part, 0)
    for sweep in range(SWEEPS):
        for step in range(1, nodes):
            value_copy(sweep, step).wait_send()
    for step in range(1, copies):
        share_copy(gradient_ref, gradient_send, gradient_recv, step).wait()
    for step in range(1, copies):
        share_copy(adjoint_ref, adjoint_send, adjoint_recv, step).wait()


def sum_and_solve(parts, neighbours, block_inverse, pair_phi, sizes):
    nodes = sizes[0]
    copies = sizes[1] * sizes[2]
    ranks, height, width = parts.shape
    own = block_inverse.shape[0]
    rows = height // own
    vmem = pl.BlockSpec(memory_space=pltpu.VMEM)
    dma = pltpu.SemaphoreType.DMA
    return pl.pallas_call(
        functools.partial(adjoint_kernel, sizes),
        in_specs=[pl.BlockSpec(memory_space=pltpu.SMEM), vmem, vmem, vmem],
        out_specs=[vmem, vmem],
        out_shape=[jax.ShapeDtypeStruct((copies, height, width), jnp.float32)] * 2,
        scratch_shapes=[
            pltpu.VMEM((ranks, height, width), jnp.bfloat16),
            pltpu.VMEM((SWEEPS, nodes, height, width), jnp.bfloat16),
            pltpu.VMEM((nodes * own, rows, width), jnp.float32),
            pltpu.VMEM((height, width), jnp.float32),
            dma((ranks,)),
            dma((ranks,)),
            dma((copies,)),
            dma((copies,)),
            dma((copies,)),
            dma((copies,)),
            dma((SWEEPS, nodes)),
            dma((SWEEPS, nodes)),
        ],
        compiler_params=pltpu.CompilerParams(
            collective_id=1, has_side_effects=True, vmem_limit_bytes=40 << 20
        ),
    )(neighbours, parts, block_inverse, pair_phi)


def local(
    sizes, volume_grad, volume_coords, support, control_coords, neighbours, block_inverse
):
    nodes = sizes[0]
    copies = sizes[1] * sizes[2]
    own, coupled = neighbours.shape
    funcs, width = volume_grad.shape[1:]
    taken = funcs // copies
    rows = max(taken, 8)
    all_centers = gather_centers(control_coords, nodes)
    partial_value = partial_gradient(volume_grad, volume_coords, support, all_centers)
    parts = partial_value.reshape(nodes, own, copies, taken, width).transpose(0, 2, 1, 3, 4)
    parts = jnp.pad(parts, ((0, 0),) * 3 + ((0, rows - taken), (0, 0)))
    parts = parts.reshape(nodes * copies, own * rows, width).astype(jnp.bfloat16)
    picks = neighbours[:, :, None] == jnp.arange(all_centers.shape[0], dtype=jnp.int32)
    near_coords = jnp.einsum(
        "ckn,ndi->ckdi", picks.astype(jnp.float32), all_centers, precision=lax.Precision.HIGHEST
    )
    pair_phi = wendland(near_coords, control_coords[:, None])
    pair_phi = pair_phi.reshape(own, coupled * width, width)
    outputs = sum_and_solve(parts, neighbours, block_inverse, pair_phi, sizes)

    def whole(shares):
        shares = shares.reshape(copies, own, rows, width)[:, :, :taken]
        return shares.transpose(1, 0, 2, 3).reshape(own, funcs, width)

    return tuple(whole(shares) for shares in outputs)


def solution(mesh):
    sizes = tuple(mesh.shape[name] for name in ("node", "fn", "sub"))
    return jax.shard_map(
        functools.partial(local, sizes),
        mesh=mesh,
        in_specs=(
            P(("sect", "node", "fn", "sub"), None, None),
            P(("sect", "node", "fn", "sub"), None, None),
            P(("sect", "node", "fn", "sub"), None),
            P(("sect", "node"), None, None),
            P(("sect", "node"), None),
            P(("sect", "node"), None, None),
        ),
        out_specs=(P(("sect", "node"), None, None), P(("sect", "node"), None, None)),
        check_vma=False,
    )
```

```python
import functools

import jax
import jax.numpy as jnp
from jax import lax
from jax.experimental import pallas as pl
from jax.experimental.pallas import tpu as pltpu
from jax.sharding import PartitionSpec as P

SWEEPS = 2


RADIUS = 1.2


DEPTH = 32


ROUND_UP = 1.0 + 2.0**-19


TINY = 1e-12


MESH = pl.DeviceIdType.MESH


def wendland(points, centers):
    diff = points[..., :, :, None] - centers[..., :, None, :]
    dist = jnp.sqrt(jnp.sum(diff * diff, axis=-3))
    ratio = dist / RADIUS
    inside = jnp.maximum(1.0 - ratio, 0.0)
    return (inside**4 * (4.0 * ratio + 1.0)).astype(jnp.bfloat16)


def cut(x, terms):
    pieces = []
    for _ in range(terms):
        piece = lax.reduce_precision(x, 8, 7)
        pieces.append(piece)
        x = x - piece
    return pieces


def factors(points, left):
    high, low = cut(points * (1.0 / RADIUS), 2)
    kept = high + low
    norm = jnp.sum(kept * kept, axis=1, keepdims=True) * ROUND_UP + TINY
    norm = jnp.concatenate(cut(norm, 3), axis=1)
    one = jnp.ones_like(norm)
    if left:
        rows = [high, low, high, low, norm, one]
    else:
        rows = [-2.0 * high, -2.0 * high, -2.0 * low, -2.0 * low, one, norm]
    used = sum(row.shape[1] for row in rows)
    rows.append(jnp.zeros((points.shape[0], DEPTH - used, points.shape[2]), jnp.float32))
    return jnp.concatenate(rows, axis=1).astype(jnp.bfloat16)


def quarter_phi(square):
    ratio = square * lax.rsqrt(square)
    inside = jnp.maximum(1.0 - ratio, 0.0)
    inside = inside * inside
    return (inside * inside * (ratio + 0.25)).astype(jnp.bfloat16)


def gradient_kernel(left_ref, right_ref, grad_ref, count_ref, out_ref, weight_ref):
    funcs = grad_ref.shape[0]
    width = out_ref.shape[2]
    pairs = right_ref.shape[0]

    @pl.when(pl.program_id(0) == 0)
    def _():
        for s in range(count_ref.shape[1]):
            column = count_ref[:, s : s + 1]
            weight_ref[:, s * width : (s + 1) * width] = jnp.broadcast_to(
                column, (column.shape[0], width)
            )

    for pair in range(pairs):
        square = jnp.dot(left_ref[...], right_ref[pair], preferred_element_type=jnp.float32)
        phi = quarter_phi(square)
        grads = grad_ref[...]
        scaled = []
        for half in range(2):
            row = weight_ref[pl.ds((pl.program_id(0) * pairs + pair) * 2 + half, 1), :]
            row = jnp.broadcast_to(row, grads.shape)
            scaled.append(grads * row.astype(jnp.bfloat16))
        both = jnp.dot(jnp.concatenate(scaled, 0), phi, preferred_element_type=jnp.float32)
        out_ref[2 * pair] = both[:funcs, :width]
        out_ref[2 * pair + 1] = both[funcs:, width:]


def partial_gradient(volume_grad, volume_coords, support, all_centers):
    blocks, funcs, width = volume_grad.shape
    control = all_centers.shape[0]
    pairs = control // 2
    together = next(n for n in (4, 2, 1) if pairs % n == 0)
    points = blocks * width
    left = factors(volume_coords, True).transpose(0, 2, 1).reshape(points, DEPTH)
    right = factors(all_centers, False).reshape(pairs, 2, DEPTH, width)
    right = right.transpose(0, 2, 1, 3).reshape(pairs, DEPTH, 2 * width)
    grads = volume_grad.transpose(1, 0, 2).reshape(funcs, points)
    listed = support[None] == jnp.arange(control, dtype=jnp.int32)[:, None, None]
    counts = 4.0 * jnp.sum(listed.astype(jnp.float32), axis=2)
    return pl.pallas_call(
        gradient_kernel,
        grid=(pairs // together,),
        in_specs=[
            pl.BlockSpec((points, DEPTH), lambda i: (0, 0)),
            pl.BlockSpec((together, DEPTH, 2 * width), lambda i: (i, 0, 0)),
            pl.BlockSpec((funcs, points), lambda i: (0, 0)),
            pl.BlockSpec((control, blocks), lambda i: (0, 0)),
        ],
        out_specs=pl.BlockSpec((2 * together, funcs, width), lambda i: (i, 0, 0)),
        out_shape=jax.ShapeDtypeStruct((control, funcs, width), jnp.float32),
        scratch_shapes=[pltpu.VMEM((control, points), jnp.float32)],
        compiler_params=pltpu.CompilerParams(vmem_limit_bytes=48 << 20),
    )(left, right, grads, counts)


def place(rank, sizes):
    copies = sizes[1] * sizes[2]
    return {
        "node": rank // copies,
        "fn": (rank % copies) // sizes[2],
        "sub": rank % sizes[2],
    }


def signal_and_wait(peers, where):
    barrier = pltpu.get_barrier_semaphore()

    def tell(step, carry):
        pl.semaphore_signal(barrier, inc=1, device_id=where(step), device_id_type=MESH)
        return carry

    lax.fori_loop(1, peers + 1, tell, 0)
    pl.semaphore_wait(barrier, peers)


def center_kernel(nodes, own_ref, all_ref, send_sem, recv_sem):
    me = lax.axis_index("node")

    def where(step):
        return {"node": (me + step) % nodes}

    signal_and_wait(nodes - 1, where)
    all_ref[me] = own_ref[...]

    def copy(step):
        return pltpu.make_async_remote_copy(
            src_ref=own_ref,
            dst_ref=all_ref.at[me],
            send_sem=send_sem.at[step],
            recv_sem=recv_sem.at[step],
            device_id=where(step),
            device_id_type=MESH,
        )

    for step in range(1, nodes):
        copy(step).start()
    for step in range(1, nodes):
        copy(step).wait()


def gather_centers(control_coords, nodes):
    own, dims, width = control_coords.shape
    gathered = pl.pallas_call(
        functools.partial(center_kernel, nodes),
        in_specs=[pl.BlockSpec(memory_space=pltpu.VMEM)],
        out_specs=pl.BlockSpec(memory_space=pltpu.VMEM),
        out_shape=jax.ShapeDtypeStruct((nodes, own * dims, width), jnp.float32),
        scratch_shapes=[
            pltpu.SemaphoreType.DMA((nodes,)),
            pltpu.SemaphoreType.DMA((nodes,)),
        ],
        compiler_params=pltpu.CompilerParams(collective_id=0, has_side_effects=True),
    )(control_coords.reshape(own * dims, width))
    return gathered.reshape(nodes * own, dims, width)


def adjoint_kernel(
    sizes,
    near_ref,
    part_ref,
    inverse_ref,
    phi_ref,
    gradient_ref,
    adjoint_ref,
    landed,
    values,
    wide,
    total,
    part_send,
    part_recv,
    gradient_send,
    gradient_recv,
    adjoint_send,
    adjoint_recv,
    value_send,
    value_recv,
):
    nodes = sizes[0]
    copies = sizes[1] * sizes[2]
    ranks = nodes * copies
    node = lax.axis_index("node")
    share = lax.axis_index("fn") * sizes[2] + lax.axis_index("sub")
    rank = node * copies + share
    own = inverse_ref.shape[0]
    rows = part_ref.shape[1] // own
    coupled = phi_ref.shape[1] // phi_ref.shape[2]
    width = phi_ref.shape[2]

    def peer(step):
        return (rank + step) % ranks

    signal_and_wait(ranks - 1, lambda step: place(peer(step), sizes))

    def part_copy(step):
        return pltpu.make_async_remote_copy(
            src_ref=part_ref.at[peer(step)],
            dst_ref=landed.at[step],
            send_sem=part_send.at[step],
            recv_sem=part_recv.at[step],
            device_id=place(peer(step), sizes),
            device_id_type=MESH,
        )

    def start_part(step, carry):
        part_copy(step).start()
        return carry

    lax.fori_loop(1, ranks, start_part, 0)
    total[...] = part_ref[rank].astype(jnp.float32)

    def add_part(step, carry):
        part_copy(step).wait_recv()
        total[...] += landed[step].astype(jnp.float32)
        return carry

    lax.fori_loop(1, ranks, add_part, 0)
    gradient_ref[share] = total[...]

    def share_copy(ref, send, recv, step):
        return pltpu.make_async_remote_copy(
            src_ref=ref.at[share],
            dst_ref=ref.at[share],
            send_sem=send.at[step],
            recv_sem=recv.at[step],
            device_id=place(node * copies + (share + step) % copies, sizes),
            device_id_type=MESH,
        )

    for step in range(1, copies):
        share_copy(gradient_ref, gradient_send, gradient_recv, step).start()

    def solve(c, coupling):
        right = total[c * rows : (c + 1) * rows, :]
        if coupling is not None:
            right = right - coupling
        return jnp.dot(
            right,
            inverse_ref[c],
            precision=lax.Precision.HIGHEST,
            preferred_element_type=jnp.float32,
        )

    def value_copy(sweep, step):
        return pltpu.make_async_remote_copy(
            src_ref=values.at[sweep, node],
            dst_ref=values.at[sweep, node],
            send_sem=value_send.at[sweep, step],
            recv_sem=value_recv.at[sweep, step],
            device_id=place(((node + step) % nodes) * copies + share, sizes),
            device_id_type=MESH,
        )

    adjoint = [solve(c, None) for c in range(own)]
    for sweep in range(SWEEPS):
        values[sweep, node] = jnp.concatenate(adjoint, 0).astype(jnp.bfloat16)
        for step in range(1, nodes):
            value_copy(sweep, step).start()
        for step in range(1, nodes):
            value_copy(sweep, step).wait_recv()
        for n in range(nodes):
            block = values[sweep, n].astype(jnp.float32)
            wide[n * own : (n + 1) * own] = block.reshape(own, rows, width)
        adjoint = []
        for c in range(own):
            near = [wide[near_ref[c, k]] for k in range(coupled)]
            near = jnp.concatenate(near, 1).astype(jnp.bfloat16)
            coupling = jnp.dot(near, phi_ref[c], preferred_element_type=jnp.float32)
            adjoint.append(solve(c, coupling))
    adjoint_ref[share] = jnp.concatenate(adjoint, 0)
    for step in range(1, copies):
        share_copy(adjoint_ref, adjoint_send, adjoint_recv, step).start()

    def end_part(step, carry):
        part_copy(step).wait_send()
        return carry

    lax.fori_loop(1, ranks, end_part, 0)
    for sweep in range(SWEEPS):
        for step in range(1, nodes):
            value_copy(sweep, step).wait_send()
    for step in range(1, copies):
        share_copy(gradient_ref, gradient_send, gradient_recv, step).wait()
    for step in range(1, copies):
        share_copy(adjoint_ref, adjoint_send, adjoint_recv, step).wait()


def sum_and_solve(parts, neighbours, block_inverse, pair_phi, sizes):
    nodes = sizes[0]
    copies = sizes[1] * sizes[2]
    ranks, height, width = parts.shape
    own = block_inverse.shape[0]
    rows = height // own
    vmem = pl.BlockSpec(memory_space=pltpu.VMEM)
    dma = pltpu.SemaphoreType.DMA
    return pl.pallas_call(
        functools.partial(adjoint_kernel, sizes),
        in_specs=[pl.BlockSpec(memory_space=pltpu.SMEM), vmem, vmem, vmem],
        out_specs=[vmem, vmem],
        out_shape=[jax.ShapeDtypeStruct((copies, height, width), jnp.float32)] * 2,
        scratch_shapes=[
            pltpu.VMEM((ranks, height, width), jnp.bfloat16),
            pltpu.VMEM((SWEEPS, nodes, height, width), jnp.bfloat16),
            pltpu.VMEM((nodes * own, rows, width), jnp.float32),
            pltpu.VMEM((height, width), jnp.float32),
            dma((ranks,)),
            dma((ranks,)),
            dma((copies,)),
            dma((copies,)),
            dma((copies,)),
            dma((copies,)),
            dma((SWEEPS, nodes)),
            dma((SWEEPS, nodes)),
        ],
        compiler_params=pltpu.CompilerParams(
            collective_id=1, has_side_effects=True, vmem_limit_bytes=40 << 20
        ),
    )(neighbours, parts, block_inverse, pair_phi)


def local(
    sizes, volume_grad, volume_coords, support, control_coords, neighbours, block_inverse
):
    nodes = sizes[0]
    copies = sizes[1] * sizes[2]
    own, coupled = neighbours.shape
    funcs, width = volume_grad.shape[1:]
    taken = funcs // copies
    rows = max(taken, 8)
    all_centers = gather_centers(control_coords, nodes)
    partial_value = partial_gradient(volume_grad, volume_coords, support, all_centers)
    parts = partial_value.reshape(nodes, own, copies, taken, width).transpose(0, 2, 1, 3, 4)
    parts = jnp.pad(parts, ((0, 0),) * 3 + ((0, rows - taken), (0, 0)))
    parts = parts.reshape(nodes * copies, own * rows, width).astype(jnp.bfloat16)
    picks = neighbours[:, :, None] == jnp.arange(all_centers.shape[0], dtype=jnp.int32)
    near_coords = jnp.einsum(
        "ckn,ndi->ckdi", picks.astype(jnp.float32), all_centers, precision=lax.Precision.HIGHEST
    )
    pair_phi = wendland(near_coords, control_coords[:, None])
    pair_phi = pair_phi.reshape(own, coupled * width, width)
    outputs = sum_and_solve(parts, neighbours, block_inverse, pair_phi, sizes)

    def whole(shares):
        shares = shares.reshape(copies, own, rows, width)[:, :, :taken]
        return shares.transpose(1, 0, 2, 3).reshape(own, funcs, width)

    return tuple(whole(shares) for shares in outputs)


def solution(mesh):
    sizes = tuple(mesh.shape[name] for name in ("node", "fn", "sub"))
    return jax.shard_map(
        functools.partial(local, sizes),
        mesh=mesh,
        in_specs=(
            P(("sect", "node", "fn", "sub"), None, None),
            P(("sect", "node", "fn", "sub"), None, None),
            P(("sect", "node", "fn", "sub"), None),
            P(("sect", "node"), None, None),
            P(("sect", "node"), None),
            P(("sect", "node"), None, None),
        ),
        out_specs=(P(("sect", "node"), None, None), P(("sect", "node"), None, None)),
        check_vma=False,
    )
```
